32 devices in a mesh: groups: 2 (over y), cells: 4 (over z), role: 2 (over x), sub: 2 (over core).
Axes of the slice: x: 2, y: 2, z: 4, core: 2. Of those that a mesh axis runs over, the one named last changes fastest.
Arguments:
- tracers: float32 [16, 80, 4096], P('sub', None, ('groups', 'cells', 'role')), parts along dimension 2, may hold values from -6 to 6
- layer_count: int32 [4096], P(('groups', 'cells', 'role')), parts along dimension 0, may hold values from 40 to 80
- neighbor: int32 [6, 4096], P(None, ('groups', 'cells', 'role')), parts along dimension 1, may hold values from 0 to 511, as said below
- halo_cells: int32 [2, 2048], P(None, ('groups', 'cells', 'role')), parts along dimension 1, may hold values from 0 to 255, as said below
- transport: float32 [80, 24576], P('sub', ('groups', 'cells', 'role')), parts along dimension 1, may hold values from -0.4 to 0.4
- edge_diff: float32 [80, 24576], P('sub', ('groups', 'cells', 'role')), parts along dimension 1, may hold values from 0.02 to 0.08
- record_dest: int32 [24576], P(('groups', 'cells', 'role')), parts along dimension 0, may hold values from 0 to 7, as said below
- record_slot: int32 [24576], P(('groups', 'cells', 'role')), parts along dimension 0, may hold values from 0 to 1535, as said below
- vert_diff: float32 [80, 4096], P(None, ('groups', 'cells', 'role')), parts along dimension 1, may hold values from 0.02 to 0.24
- half_sat: float32 [16], replicated, may hold values from 0.1 to 2
- stoich: float32 [16, 16], replicated, may hold values from -1.5 to 1.5
Outputs:
- tracers_next: float32 [16, 80, 4096], P('sub', None, ('groups', 'cells', 'role')), parts along dimension 2
The draws below stay inside these ranges and needn't reach their ends.
There are 2 independent parts, one for each index of `groups`. The reference program is written for one: setup_inputs(seed, part) draws one part's arguments, and reference() takes and returns one part's arrays. A program takes and returns all parts, laid end to end along the dimension named above; an argument that names none is the same for every part. Nothing has to cross between parts.
Inputs may be any that keep to these rules, and one draw needn't show every extreme that they name: `neighbor`: the cells form a hexagonal mesh of rows of 128 cells, periodic in both directions, 2 rows to a block; the neighbour relation is symmetric. An index below 256 is a cell of the same block, the others address the adjacent blocks' halo_cells lists as the steps say. `halo_cells`: for each block, two lists of 128 distinct local cells: first the cells that the previous block reads, then those that the next block reads. `record_dest`: among the records of one device, no block is named more than 384 times, and in every draw each device names some block exactly 384 times; every block is named by 1536 records in all. `record_slot`: every pair of a block and a slot is named by exactly one record.
All inputs are finite; a program needn't handle non-finite values.
Results may differ from the reference program's by a relative error of at most 0.00005.
Values sent between devices are 32-bit elements; how exact they have to be, the bound alone decides.
A program may use at most 128 MiB of HBM per device.

```python
import math
import jax
import jax.numpy as jnp
from jax import lax

NT = 16
L = 80
NCOLS = 128
ROWS_DEV = 2
CELLS_DEV = 256
BLOCKS = 8
CELLS = 2048
RECS = 12288
CAP = 384
N_CELLS = 4
N_ROLE = 2


def cell_tables(key):
    subkey = jax.random.fold_in(key, 11)
    layouts = jax.vmap(lambda one_key: jax.random.permutation(one_key, CELLS_DEV))(jax.random.split(subkey, BLOCKS)).astype(jnp.int32)
    total_rows = ROWS_DEV * BLOCKS
    row_index = jnp.broadcast_to(jnp.arange(total_rows, dtype=jnp.int32)[:, None], (total_rows, NCOLS))
    col_index = jnp.broadcast_to(jnp.arange(NCOLS, dtype=jnp.int32)[None, :], (total_rows, NCOLS))
    home_block = row_index // ROWS_DEV
    local_id = layouts[home_block, (row_index - home_block * ROWS_DEV) * NCOLS + col_index]
    global_id = home_block * CELLS_DEV + local_id
    shifted = col_index - 1 + row_index % 2
    step_list = [(0, col_index + 1), (0, col_index - 1), (1, shifted), (1, shifted + 1), (-1, shifted), (-1, shifted + 1)]
    entries = []
    for row_step, column in step_list:
        other_row = (row_index + row_step) % total_rows
        other_col = column % NCOLS
        other_home = other_row // ROWS_DEV
        other_local = layouts[other_home, (other_row - other_home * ROWS_DEV) * NCOLS + other_col]
        if row_step == 1:
            outside = CELLS_DEV + NCOLS + other_col
        elif row_step == -1:
            outside = CELLS_DEV + other_col
        else:
            outside = other_local
        entries.append(jnp.where(other_home == home_block, other_local, outside))
    ext_table = jnp.stack(entries).reshape(6, -1).astype(jnp.int32)
    neighbor = jnp.zeros((6, CELLS), jnp.int32).at[:, global_id.reshape(-1)].set(ext_table)
    halo_rows = jnp.stack([layouts[:, :NCOLS], layouts[:, (ROWS_DEV - 1) * NCOLS:]]).reshape(2, -1).astype(jnp.int32)
    return (neighbor, halo_rows)


def record_tables(key):
    subkey = jax.random.fold_in(key, 23)
    keys = jax.random.split(subkey, 4)
    per_device = 6 * CELLS_DEV
    halves = jax.random.randint(keys[0], (BLOCKS // 2,), 0, CAP + 1, dtype=jnp.int32).at[0].set(CAP)
    counts = jnp.stack([halves, CAP - halves], axis=1).reshape(-1)[jax.random.permutation(keys[1], BLOCKS)]
    starts = jnp.concatenate([jnp.zeros((1,), jnp.int32), jnp.cumsum(counts)[:-1].astype(jnp.int32)])
    position = jnp.arange(per_device, dtype=jnp.int32)
    offset = (jnp.searchsorted(starts, position, side='right') - 1).astype(jnp.int32)
    source = jnp.arange(BLOCKS, dtype=jnp.int32)[:, None]
    targets = (source + offset[None, :]) % BLOCKS
    orders = jax.vmap(lambda one_key: jax.random.permutation(one_key, per_device))(jax.random.split(keys[2], BLOCKS)).astype(jnp.int32)
    slots = orders[targets, position[None, :]]
    shuffle = jax.vmap(lambda one_key: jax.random.permutation(one_key, per_device))(jax.random.split(keys[3], BLOCKS)).astype(jnp.int32)
    targets = jnp.take_along_axis(targets, shuffle, axis=1)
    slots = jnp.take_along_axis(slots, shuffle, axis=1)
    return (targets.reshape(-1).astype(jnp.int32), slots.reshape(-1).astype(jnp.int32))


def draw_neighbor(key, part):
    return cell_tables(key)[0]


def draw_halo_cells(key, part):
    return cell_tables(key)[1]


def draw_record_dest(key, part):
    return record_tables(key)[0]


def draw_record_slot(key, part):
    return record_tables(key)[1]


def touch_ends(values, key, least, largest):
    place = [jax.random.randint(jax.random.fold_in(key, axis), (), 0, length) for axis, length in enumerate(values.shape)]
    longest = values.shape.index(max(values.shape))
    next_to = place[:longest] + [(place[longest] + 1) % values.shape[longest]] + place[longest + 1:]
    return values.at[tuple(place)].set(least).at[tuple(next_to)].set(largest)


def steps_of(stream_key, extent, cuts, least, largest):
    loudness, own = 1.0, jax.random.fold_in(stream_key, 6)
    for dim, blocks in cuts:
        steps = jnp.exp(jax.random.uniform(jax.random.fold_in(own, dim), (blocks,), jnp.float32, least / len(cuts), largest / len(cuts)))
        loudness = loudness * jnp.repeat(steps, extent[dim] // blocks).reshape([-1 if axis == dim else 1 for axis in range(len(extent))])
    return loudness


def noise(key, dims, width, limit, cuts=(), held_as=jnp.bfloat16):
    level = steps_of(key, dims, cuts, -0.22, 0.18) if cuts else 1.0
    drawn = jax.random.normal(key, dims, jnp.float32) * width * level
    return jnp.minimum(jnp.maximum(drawn, -limit), limit).astype(held_as)


def setup_inputs(seed: int = 0, part: int = 0) -> dict:
    key_of = jax.random.split(jax.random.key(seed), 12)
    own_keys = jax.random.split(jax.random.fold_in(key_of[11], part), 12)
    return {
        "tracers": noise(own_keys[0], (NT, L, CELLS), 1.0, 6.0, ((0, 2), (2, 8)), jnp.float32),
        "layer_count": touch_ends(jax.random.randint(own_keys[1], (CELLS,), L // 2, L + 1), jax.random.fold_in(own_keys[1], 1), L // 2, L).astype(jnp.int32),
        "neighbor": draw_neighbor(jax.random.fold_in(jax.random.fold_in(key_of[11], part), 71), part),
        "halo_cells": draw_halo_cells(jax.random.fold_in(jax.random.fold_in(key_of[11], part), 71), part),
        "transport": jnp.clip(jax.random.uniform(own_keys[4], (L, RECS), jnp.float32, -0.4, 0.4) * steps_of(own_keys[4], (L, RECS), ((0, 2), (1, 8)), -0.4, 0.0), -0.4, 0.4),
        "edge_diff": jnp.clip(0.02 + 0.06 * jax.random.uniform(own_keys[5], (L, RECS), jnp.float32) ** steps_of(own_keys[5], (L, RECS), ((0, 2), (1, 8)), -0.2, 0.2), 0.02, 0.08),
        "record_dest": draw_record_dest(jax.random.fold_in(jax.random.fold_in(key_of[11], part), 71), part),
        "record_slot": draw_record_slot(jax.random.fold_in(jax.random.fold_in(key_of[11], part), 71), part),
        "vert_diff": jnp.clip(0.02 + 0.22 * jax.random.uniform(own_keys[8], (L, CELLS), jnp.float32) ** steps_of(own_keys[8], (L, CELLS), ((1, 8),), -0.2, 0.2), 0.02, 0.24),
        "half_sat": jnp.clip(jnp.exp(jax.random.uniform(key_of[9], (NT,), jnp.float32, math.log(0.1), math.log(2.0))), 0.1, 2.0),
        "stoich": noise(key_of[10], (NT, NT), NT ** -0.5, 1.5, (), jnp.float32),
    }


LIMIT_PAD = 1.5
REACT_RATE = 0.5


def edge_terms(field, beyond, open_mask, flow, kappa):
    upwind = open_mask * (jnp.maximum(flow, 0.0) * field + jnp.minimum(flow, 0.0) * beyond)
    antidiff = open_mask * (0.5 * flow * (field + beyond)) - upwind
    diffuse = open_mask * kappa * (beyond - field)
    return upwind, antidiff, diffuse


def column_mix(advected, vert_diff, wet_mask):
    coupling = vert_diff[:-1] * wet_mask[:-1] * wet_mask[1:]
    vertical = coupling * (advected[..., 1:, :] - advected[..., :-1, :])
    zero_layer = jnp.zeros_like(advected[..., :1, :])
    return advected + jnp.concatenate([vertical, zero_layer], axis=-2) - jnp.concatenate([zero_layer, vertical], axis=-2)


def reference(tracers, layer_count, neighbor, halo_cells, transport, edge_diff, record_dest, record_slot, vert_diff, half_sat, stoich):
    blocks = N_CELLS * N_ROLE
    extended = neighbor.reshape(6, blocks, CELLS_DEV)
    block_index = jnp.arange(blocks, dtype=jnp.int32)[None, :, None]
    below_block = (block_index - 1) % blocks
    above_block = (block_index + 1) % blocks
    top_rows = halo_cells[1].reshape(blocks, NCOLS)
    bottom_rows = halo_cells[0].reshape(blocks, NCOLS)
    from_below = below_block * CELLS_DEV + top_rows[below_block, jnp.clip(extended - CELLS_DEV, 0, NCOLS - 1)]
    from_above = above_block * CELLS_DEV + bottom_rows[above_block, jnp.clip(extended - CELLS_DEV - NCOLS, 0, NCOLS - 1)]
    inside_id = block_index * CELLS_DEV + extended
    global_nb = jnp.where(extended < CELLS_DEV, inside_id, jnp.where(extended < CELLS_DEV + NCOLS, from_below, from_above))
    global_nb = global_nb.reshape(6, CELLS).astype(jnp.int32)
    positions = (record_dest * (6 * CELLS_DEV) + record_slot).astype(jnp.int32)
    flow_table = jnp.zeros((L, RECS), jnp.float32).at[:, positions].set(transport)
    kappa_table = jnp.zeros((L, RECS), jnp.float32).at[:, positions].set(edge_diff)
    flow_edges = flow_table.reshape(L, blocks, 6, CELLS_DEV).transpose(2, 0, 1, 3).reshape(6, L, CELLS)
    kappa_edges = kappa_table.reshape(L, blocks, 6, CELLS_DEV).transpose(2, 0, 1, 3).reshape(6, L, CELLS)
    wet_mask = (jnp.arange(L, dtype=jnp.int32)[:, None] < layer_count[None, :]).astype(jnp.float32)

    def advect_one(field):
        total_abs = jnp.zeros_like(field)
        upper_bound = field
        lower_bound = field
        for slot_index in range(6):
            nb_cells = global_nb[slot_index]
            beyond = field[:, nb_cells]
            open_mask = wet_mask * wet_mask[:, nb_cells]
            upwind, antidiff, diffuse = edge_terms(field, beyond, open_mask, flow_edges[slot_index], kappa_edges[slot_index])
            total_abs = total_abs + jnp.abs(antidiff)
            candidate = jnp.where(open_mask > 0, beyond, field)
            upper_bound = jnp.maximum(upper_bound, candidate)
            lower_bound = jnp.minimum(lower_bound, candidate)
        spread = upper_bound - lower_bound
        limiter_ratio = spread / (spread + total_abs + LIMIT_PAD)
        net_flux = jnp.zeros_like(field)
        for slot_index in range(6):
            nb_cells = global_nb[slot_index]
            beyond = field[:, nb_cells]
            open_mask = wet_mask * wet_mask[:, nb_cells]
            upwind, antidiff, diffuse = edge_terms(field, beyond, open_mask, flow_edges[slot_index], kappa_edges[slot_index])
            bound = jnp.minimum(limiter_ratio, limiter_ratio[:, nb_cells])
            net_flux = net_flux + (upwind + bound * antidiff - diffuse)
        return column_mix(field - net_flux, vert_diff, wet_mask)

    mixed_field = lax.map(advect_one, tracers)
    uptake = mixed_field * mixed_field / (half_sat[:, None, None] + mixed_field * mixed_field)
    reaction = jnp.einsum("ij,jlc->ilc", stoich, uptake, precision=lax.Precision.HIGHEST)
    sunlight = jnp.exp(-3.0 * jnp.arange(L, dtype=jnp.float32) / L)
    return mixed_field + REACT_RATE * (sunlight[:, None] * wet_mask)[None] * reaction
```

```python
import functools

import jax
import jax.numpy as jnp
from jax import lax
from jax.experimental import pallas as pl
from jax.experimental.pallas import tpu as pltpu
from jax.sharding import PartitionSpec as P

LIMIT_PAD = 1.5
REACT_RATE = 0.5
F32 = jnp.float32
BF16 = jnp.bfloat16
MESH = pl.DeviceIdType.MESH
NT_DIMS = (((1,), (1,)), ((), ()))


def steps(count, fn):
    if count <= 8:
        for i in range(count):
            fn(i)
    else:
        lax.fori_loop(0, count, lambda i, c: (fn(i), c)[1], 0)


def dot(a, b):
    return jnp.dot(a, b, preferred_element_type=F32)


def dot_nt(a, b):
    return lax.dot_general(a, b, NT_DIMS, preferred_element_type=F32)


def split(x):
    hi = x.astype(BF16)
    return hi, (x - hi.astype(F32)).astype(BF16)


def onehot(cond):
    return jnp.where(cond, 1.0, 0.0).astype(BF16)


def kernel(
    blocks, n_role, cap,
    tr_ref, lc_ref, nb_ref, halo_ref, tp_ref, ed_ref, dest_ref, slot_ref, vd_ref,
    hs_ref, st_ref,
    out_ref,
    field, rec_a, send, arrived, flow, xa, la, gsel, hsel, pk, lk, lim, adv, edge_out, edge_in,
    rim_out, rim_in, lrim_out, lrim_in, res, masks, terms,
    send_sem, recv_sem, tr_sem, rim_send, rim_recv, lrim_send, lrim_recv, edge_sem, res_sem,
):
    own, layers, cells = tr_ref.shape
    half = layers // 2
    tracers = 2 * own
    rows = tracers * half
    cols = halo_ref.shape[1]
    ext = cells + 2 * cols
    recs = dest_ref.shape[1]
    slots = 6 * cells
    sub = lax.axis_index("sub")
    me = lax.axis_index("cells") * n_role + lax.axis_index("role")
    other = {"sub": 1 - sub}

    def at(block):
        return {"cells": block // n_role, "role": lax.rem(block, n_role)}

    def partner(d):
        return lax.rem(me + d, blocks)

    barrier = pltpu.get_barrier_semaphore()

    def greet(i):
        pl.semaphore_signal(barrier, inc=1, device_id=at(partner(i + 1)), device_id_type=MESH)

    steps(blocks - 1, greet)
    pl.semaphore_signal(barrier, inc=1, device_id=other, device_id_type=MESH)
    pl.semaphore_wait(barrier, blocks)

    mine = pl.multiple_of(sub * half, half)
    theirs = pl.multiple_of((1 - sub) * half, half)

    tr_copy = pltpu.make_async_remote_copy(
        src_ref=tr_ref.at[:, pl.ds(theirs, half), :],
        dst_ref=field.at[pl.ds(sub * own, own)],
        send_sem=tr_sem.at[0], recv_sem=tr_sem.at[1],
        device_id=other, device_id_type=MESH,
    )
    tr_copy.start()

    dest = dest_ref[...]
    block_id = lax.broadcasted_iota(jnp.int32, (max(blocks, 8), recs), 0)
    match = jnp.where(block_id == dest, 1.0, 0.0)
    chunk = 256
    before = onehot(
        lax.broadcasted_iota(jnp.int32, (chunk, chunk), 0)
        < lax.broadcasted_iota(jnp.int32, (chunk, chunk), 1)
    )
    carry = jnp.zeros((match.shape[0], 1), F32)
    ranks = []
    for c in range(recs // chunk):
        part = match[:, c * chunk:(c + 1) * chunk]
        rank = dot(part.astype(BF16), before) + carry
        ranks.append(jnp.sum(rank * part, axis=0, keepdims=True))
        carry = carry + jnp.sum(part, axis=1, keepdims=True)
    rank = jnp.concatenate(ranks, axis=1).astype(jnp.int32)
    target = dest * cap + rank

    slot_rows = jnp.broadcast_to(slot_ref[...].astype(F32) + 1.0, (8, recs))
    payload = jnp.concatenate([tp_ref[...], ed_ref[...], slot_rows], axis=0)
    width = payload.shape[0]
    top = payload.astype(BF16).astype(F32)
    rec_a[...] = jnp.concatenate([top, payload - top], axis=0).astype(BF16)

    place = lax.broadcasted_iota(jnp.int32, (cap, recs), 0)

    def pack(block):
        sel = onehot(place == target - block * cap)
        both = dot_nt(rec_a[...], sel)
        return both[:width] + both[width:]

    def rec_copy(block, source):
        return pltpu.make_async_remote_copy(
            src_ref=send.at[block], dst_ref=arrived.at[source],
            send_sem=send_sem.at[block], recv_sem=recv_sem.at[source],
            device_id=at(block), device_id_type=MESH,
        )

    order = (4, 3, 5, 2, 6, 1, 7)

    def offset(i):
        return order[i] if blocks == 8 else i + 1

    def ship(i):
        block = partner(offset(i))
        send[block] = pack(block)
        rec_copy(block, me).start()

    steps(blocks - 1, ship)
    arrived[me] = pack(me)

    local_rows = lax.broadcasted_iota(jnp.int32, (cells, cols), 0)
    for side in range(2):
        sel = onehot(local_rows == halo_ref[side:side + 1, :])
        hsel[0:cells, side * cols:(side + 1) * cols] = sel
        hsel[cells:2 * cells, side * cols:(side + 1) * cols] = sel
    ext_rows = lax.broadcasted_iota(jnp.int32, (ext, cells), 0)
    for k in range(6):
        sel = onehot(ext_rows == nb_ref[k:k + 1, :])
        gsel[k, 0:ext, :] = sel
        gsel[k, ext:2 * ext, :] = sel

    field[pl.ds(sub * own, own)] = tr_ref[:, pl.ds(mine, half), :]
    tr_copy.wait()
    whole = field[...].reshape(rows, cells)
    hi, lo = split(whole)
    xa[:, 0:cells] = hi
    xa[:, ext:ext + cells] = lo
    picked = dot(hi, hsel[0:cells]) + dot(lo, hsel[cells:2 * cells])
    count = jnp.broadcast_to(lc_ref[...].astype(F32), (8, cells))
    picked_count = dot(count.astype(BF16), hsel[0:cells])
    for side in range(2):
        rim_out[side, 0:rows] = picked[:, side * cols:(side + 1) * cols]
        rim_out[side, rows:rows + 8] = picked_count[:, side * cols:(side + 1) * cols]

    def rim_copies(out, into, s_sem, r_sem):
        result = []
        for side in range(2):
            to = partner(blocks - 1 if side == 0 else 1)
            result.append(pltpu.make_async_remote_copy(
                src_ref=out.at[side], dst_ref=into.at[1 - side],
                send_sem=s_sem.at[side], recv_sem=r_sem.at[1 - side],
                device_id=at(to), device_id_type=MESH,
            ))
        return result

    rims = rim_copies(rim_out, rim_in, rim_send, rim_recv)
    for copy in rims:
        copy.start()
    for copy in rims:
        copy.wait_recv()

    layer = lax.broadcasted_iota(jnp.int32, (half, cells), 0) + sub * half
    wet = jnp.where(layer < lc_ref[...], 1.0, 0.0)
    layer_f = layer.astype(F32)
    count_ext = jnp.concatenate(
        [count, rim_in[0, rows:rows + 8], rim_in[1, rows:rows + 8]], axis=1
    ).astype(BF16)
    for side in range(2):
        hi, lo = split(rim_in[side, 0:rows])
        first = cells + side * cols
        xa[:, first:first + cols] = hi
        xa[:, ext + first:ext + first + cols] = lo
    for k in range(6):
        pk[k] = dot(xa[...], gsel[k])
        far_count = dot(count_ext, gsel[k, 0:ext])[0:1]
        masks[k] = jnp.where(layer_f < far_count, wet, 0.0)

    flow[...] = jnp.zeros_like(flow)
    slot_id = lax.broadcasted_iota(jnp.int32, (slots, cap), 0).astype(F32) + 1.0

    def unpack(block):
        got = arrived[block]
        sel = onehot(slot_id == got[width - 8:width - 7, :])
        body = got[:width - 8]
        top = body.astype(BF16).astype(F32)
        both = dot_nt(jnp.concatenate([top, body - top], axis=0).astype(BF16), sel)
        flow[...] += both[:width - 8] + both[width - 8:]

    unpack(me)

    def take(i):
        block = partner(blocks - offset(i))
        rec_copy(block, block).wait_recv()
        unpack(block)

    steps(blocks - 1, take)

    total = jnp.zeros((half, cells), F32)
    for k in range(6):
        u = flow[0:half, k * cells:(k + 1) * cells] * masks[k]
        kap = flow[half:2 * half, k * cells:(k + 1) * cells] * masks[k]
        terms[k] = 0.5 * jnp.abs(u)
        terms[6 + k] = jnp.minimum(u, 0.0) - kap
        total = total + u
    terms[12] = total

    def limiter(t, c):
        q = field[t]
        here = pl.ds(pl.multiple_of(t * half, half), half)
        high = jnp.zeros_like(q)
        low = jnp.zeros_like(q)
        size = jnp.zeros_like(q)
        for k in range(6):
            d = (pk[k, here, :] - q) * masks[k]
            pk[k, here, :] = d
            high = jnp.maximum(high, d)
            low = jnp.minimum(low, d)
            size = size + terms[k] * jnp.abs(d)
        spread = high - low
        lim[here, :] = spread / (spread + size + LIMIT_PAD)
        return c

    lax.fori_loop(0, tracers, limiter, 0)

    hi, lo = split(lim[...])
    la[:, 0:cells] = hi
    la[:, ext:ext + cells] = lo
    picked = dot(hi, hsel[0:cells]) + dot(lo, hsel[cells:2 * cells])
    for side in range(2):
        lrim_out[side] = picked[:, side * cols:(side + 1) * cols]
    lrims = rim_copies(lrim_out, lrim_in, lrim_send, lrim_recv)
    for copy in lrims:
        copy.start()
    for copy in lrims:
        copy.wait_recv()
    for side in range(2):
        hi, lo = split(lrim_in[side])
        first = cells + side * cols
        la[:, first:first + cols] = hi
        la[:, ext + first:ext + first + cols] = lo
    for k in range(6):
        lk[k] = dot(la[...], gsel[k])

    def advect(t, c):
        q = field[t]
        here = pl.ds(pl.multiple_of(t * half, half), half)
        own_lim = lim[here, :]
        net = q * terms[12]
        for k in range(6):
            bound = jnp.minimum(own_lim, lk[k, here, :])
            net = net + pk[k, here, :] * (terms[6 + k] + bound * terms[k])
        adv[t] = q - net
        return c

    lax.fori_loop(0, tracers, advect, 0)

    @pl.when(sub == 0)
    def _():
        edge_out[...] = adv[:, half - 1, :]

    @pl.when(sub == 1)
    def _():
        edge_out[...] = adv[:, 0, :]

    edge_copy = pltpu.make_async_remote_copy(
        src_ref=edge_out, dst_ref=edge_in, send_sem=edge_sem.at[0], recv_sem=edge_sem.at[1],
        device_id=other, device_id_type=MESH,
    )
    edge_copy.start()
    edge_copy.wait()

    counts = lc_ref[...]
    upper = vd_ref[pl.ds(mine, half), :]
    w_down = jnp.where(
        (layer < layers - 1) & (layer + 1 < counts), upper, 0.0
    )
    cut = jnp.where(half < counts, vd_ref[half - 1:half, :], 0.0)
    row = lax.broadcasted_iota(jnp.int32, (half, cells), 0)
    w_up = jnp.where(row == 0, jnp.where(sub == 0, 0.0, cut), pltpu.roll(w_down, 1, 0))
    light = REACT_RATE * jnp.exp(-3.0 * layer_f / layers) * wet

    def mix(t, c):
        a = adv[t]
        across = edge_in[pl.ds(t, 1), :]
        below = jnp.where(row == half - 1, across, pltpu.roll(a, half - 1, 0))
        above = jnp.where(row == 0, across, pltpu.roll(a, 1, 0))
        m = a + w_down * (below - a) - w_up * (a - above)
        adv[t] = m
        sq = m * m
        field[t] = sq / (hs_ref[t] + sq)
        return c

    lax.fori_loop(0, tracers, mix, 0)

    def react(t):
        acc = st_ref[t, 0] * field[0]
        for s in range(1, tracers):
            acc = acc + st_ref[t, s] * field[s]
        return adv[t] + light * acc

    def far(i, c):
        res[i] = react((1 - sub) * own + i)
        return c

    def near(i, c):
        out_ref[i, pl.ds(mine, half), :] = react(sub * own + i)
        return c

    lax.fori_loop(0, own, far, 0)
    res_copy = pltpu.make_async_remote_copy(
        src_ref=res, dst_ref=out_ref.at[:, pl.ds(mine, half), :],
        send_sem=res_sem.at[0], recv_sem=res_sem.at[1],
        device_id=other, device_id_type=MESH,
    )
    res_copy.start()
    lax.fori_loop(0, own, near, 0)
    res_copy.wait()

    def drain(i):
        rec_copy(partner(i + 1), me).wait_send()

    steps(blocks - 1, drain)
    for copy in rims + lrims:
        copy.wait_send()


def body(
    tracers, layer_count, neighbor, halo_cells, transport, edge_diff,
    record_dest, record_slot, vert_diff, half_sat, stoich,
):
    own, layers, cells = tracers.shape
    half = layers // 2
    count = 2 * own
    rows = count * half
    cols = halo_cells.shape[1]
    recs = record_dest.shape[0]
    ext = cells + 2 * cols
    n_role = lax.axis_size("role")
    blocks = lax.axis_size("cells") * n_role
    cap = -(-(2 * recs // blocks) // 128) * 128
    width = layers + 8
    vmem = pl.BlockSpec(memory_space=pltpu.VMEM)
    smem = pl.BlockSpec(memory_space=pltpu.SMEM)
    pair = pltpu.SemaphoreType.DMA((2,))
    return pl.pallas_call(
        functools.partial(kernel, blocks, n_role, cap),
        out_shape=jax.ShapeDtypeStruct(tracers.shape, F32),
        in_specs=[vmem] * 9 + [smem] * 2,
        out_specs=vmem,
        scratch_shapes=[
            pltpu.VMEM((count, half, cells), F32),
            pltpu.VMEM((2 * width, recs), BF16),
            pltpu.VMEM((blocks, width, cap), F32),
            pltpu.VMEM((blocks, width, cap), F32),
            pltpu.VMEM((layers, 6 * cells), F32),
            pltpu.VMEM((rows, 2 * ext), BF16),
            pltpu.VMEM((rows, 2 * ext), BF16),
            pltpu.VMEM((6, 2 * ext, cells), BF16),
            pltpu.VMEM((2 * cells, 2 * cols), BF16),
            pltpu.VMEM((6, rows, cells), F32),
            pltpu.VMEM((6, rows, cells), F32),
            pltpu.VMEM((rows, cells), F32),
            pltpu.VMEM((count, half, cells), F32),
            pltpu.VMEM((count, cells), F32),
            pltpu.VMEM((count, cells), F32),
            pltpu.VMEM((2, rows + 8, cols), F32),
            pltpu.VMEM((2, rows + 8, cols), F32),
            pltpu.VMEM((2, rows, cols), F32),
            pltpu.VMEM((2, rows, cols), F32),
            pltpu.VMEM((own, half, cells), F32),
            pltpu.VMEM((6, half, cells), F32),
            pltpu.VMEM((13, half, cells), F32),
            pltpu.SemaphoreType.DMA((blocks,)),
            pltpu.SemaphoreType.DMA((blocks,)),
            pair, pair, pair, pair, pair, pair, pair,
        ],
        compiler_params=pltpu.CompilerParams(
            collective_id=0, has_side_effects=True, vmem_limit_bytes=52 * 1024 * 1024
        ),
        name="tracer_step",
    )(
        tracers, layer_count.reshape(1, -1), neighbor, halo_cells, transport, edge_diff,
        record_dest.reshape(1, -1), record_slot.reshape(1, -1), vert_diff, half_sat, stoich,
    )


def solution(mesh):
    in_specs = (
        P("sub", None, ("groups", "cells", "role")),
        P(("groups", "cells", "role")),
        P(None, ("groups", "cells", "role")),
        P(None, ("groups", "cells", "role")),
        P("sub", ("groups", "cells", "role")),
        P("sub", ("groups", "cells", "role")),
        P(("groups", "cells", "role")),
        P(("groups", "cells", "role")),
        P(None, ("groups", "cells", "role")),
        P(),
        P(),
    )
    out_specs = P("sub", None, ("groups", "cells", "role"))
    return jax.shard_map(body, mesh=mesh, in_specs=in_specs, out_specs=out_specs, check_vma=False)
```

```python
import functools

import jax
import jax.numpy as jnp
from jax import lax
from jax.experimental import pallas as pl
from jax.experimental.pallas import tpu as pltpu
from jax.sharding import PartitionSpec as P

LIMIT_PAD = 1.5
REACT_RATE = 0.5
F32 = jnp.float32
BF16 = jnp.bfloat16
MESH = pl.DeviceIdType.MESH
NT_DIMS = (((1,), (1,)), ((), ()))


LANES = 128


def steps(count, fn, start=0):
    if count <= 8:
        for i in range(start, count):
            fn(i)
    else:
        lax.fori_loop(start, count, lambda i, c: (fn(i), c)[1], 0)


def dot(a, b):
    return jnp.dot(a, b, preferred_element_type=F32)


def dot_nt(a, b):
    return lax.dot_general(a, b, NT_DIMS, preferred_element_type=F32)


def split(x):
    hi = x.astype(BF16)
    return hi, (x - hi.astype(F32)).astype(BF16)


def onehot(cond):
    return jnp.where(cond, 1.0, 0.0).astype(BF16)


def kernel(
    blocks, n_role, cap,
    tr_ref, lc_ref, nb_ref, halo_ref, tp_ref, ed_ref, dest_ref, slot_ref, vd_ref,
    hs_ref, st_ref,
    out_ref,
    field, rec_a, send, arrived, flow, xa, la, gsel, hsel, pk, lk, lim, adv, edge_out, edge_in,
    rim_out, rim_in, lrim_out, lrim_in, res, masks, terms,
    send_sem, recv_sem, tr_sem, rim_send, rim_recv, lrim_send, lrim_recv, edge_sem, res_sem,
):
    own, layers, cells = tr_ref.shape
    half = layers // 2
    tracers = 2 * own
    rows = tracers * half
    cols = halo_ref.shape[1]
    ext = cells + 2 * cols
    recs = dest_ref.shape[1]
    slots = 6 * cells
    sub = lax.axis_index("sub")
    me = lax.axis_index("cells") * n_role + lax.axis_index("role")
    other = {"sub": 1 - sub}

    def at(block):
        return {"cells": block // n_role, "role": lax.rem(block, n_role)}

    def partner(d):
        return lax.rem(me + d, blocks)

    barrier = pltpu.get_barrier_semaphore()

    def greet(i):
        pl.semaphore_signal(barrier, inc=1, device_id=at(partner(i + 1)), device_id_type=MESH)

    steps(blocks - 1, greet)
    pl.semaphore_signal(barrier, inc=1, device_id=other, device_id_type=MESH)
    pl.semaphore_wait(barrier, blocks)

    mine = pl.multiple_of(sub * half, half)
    theirs = pl.multiple_of((1 - sub) * half, half)

    tr_copy = pltpu.make_async_remote_copy(
        src_ref=tr_ref.at[:, pl.ds(theirs, half), :],
        dst_ref=field.at[pl.ds(sub * own, own)],
        send_sem=tr_sem.at[0], recv_sem=tr_sem.at[1],
        device_id=other, device_id_type=MESH,
    )
    tr_copy.start()

    dest = dest_ref[...]
    block_id = lax.broadcasted_iota(jnp.int32, (max(blocks, 8), recs), 0)
    match = jnp.where(block_id == dest, 1.0, 0.0)
    chunk = 256
    before = onehot(
        lax.broadcasted_iota(jnp.int32, (chunk, chunk), 0)
        < lax.broadcasted_iota(jnp.int32, (chunk, chunk), 1)
    )
    carry = jnp.zeros((match.shape[0], 1), F32)
    ranks = []
    for c in range(recs // chunk):
        part = match[:, c * chunk:(c + 1) * chunk]
        rank = dot(part.astype(BF16), before) + carry
        ranks.append(jnp.sum(rank * part, axis=0, keepdims=True))
        carry = carry + jnp.sum(part, axis=1, keepdims=True)
    rank = jnp.concatenate(ranks, axis=1).astype(jnp.int32)
    target = dest * cap + rank

    slot_rows = jnp.broadcast_to(slot_ref[...].astype(F32) + 1.0, (8, recs))
    payload = jnp.concatenate([tp_ref[...], ed_ref[...], slot_rows], axis=0)
    width = payload.shape[0]
    top = payload.astype(BF16).astype(F32)
    rec_a[...] = jnp.concatenate([top, payload - top], axis=0).astype(BF16)

    place = lax.broadcasted_iota(jnp.int32, (cap, recs), 0)

    pieces = cap // LANES
    slot_row = lax.broadcasted_iota(jnp.int32, (8, LANES), 0)

    def pack(block, ref):
        sel = onehot(place == target - block * cap)
        both = dot_nt(rec_a[...], sel)
        got = both[:width] + both[width:]
        tile = jnp.zeros((8, LANES), F32)
        for i in range(pieces):
            piece = slice(i * LANES, (i + 1) * LANES)
            ref[block, i * layers:(i + 1) * layers, :] = got[:layers, piece]
            tile = jnp.where(slot_row == i, got[layers:layers + 8, piece], tile)
        ref[block, pieces * layers:pieces * layers + 8, :] = tile

    def rec_copy(block, source):
        return pltpu.make_async_remote_copy(
            src_ref=send.at[block], dst_ref=arrived.at[source],
            send_sem=send_sem.at[block], recv_sem=recv_sem.at[source],
            device_id=at(block), device_id_type=MESH,
        )

    order = (4, 3, 5, 2, 6, 1, 7)

    def offset(i):
        return order[i] if blocks == 8 else i + 1

    def ship(i):
        block = partner(offset(i))
        pack(block, send)
        rec_copy(block, me).start()

    early = 3 if blocks == 8 else 0
    for i in range(early):
        ship(i)

    local_rows = lax.broadcasted_iota(jnp.int32, (cells, cols), 0)
    for side in range(2):
        sel = onehot(local_rows == halo_ref[side:side + 1, :])
        hsel[0:cells, side * cols:(side + 1) * cols] = sel
        hsel[cells:2 * cells, side * cols:(side + 1) * cols] = sel

    field[pl.ds(sub * own, own)] = tr_ref[:, pl.ds(mine, half), :]
    tr_copy.wait()
    whole = field[...].reshape(rows, cells)
    hi, lo = split(whole)
    xa[:, 0:cells] = hi
    xa[:, ext:ext + cells] = lo
    picked = dot(hi, hsel[0:cells]) + dot(lo, hsel[cells:2 * cells])
    count = jnp.broadcast_to(lc_ref[...].astype(F32), (8, cells))
    picked_count = dot(count.astype(BF16), hsel[0:cells])
    for side in range(2):
        rim_out[side, 0:rows] = picked[:, side * cols:(side + 1) * cols]
        rim_out[side, rows:rows + 8] = picked_count[:, side * cols:(side + 1) * cols]

    def rim_copies(out, into, s_sem, r_sem):
        result = []
        for side in range(2):
            to = partner(blocks - 1 if side == 0 else 1)
            result.append(pltpu.make_async_remote_copy(
                src_ref=out.at[side], dst_ref=into.at[1 - side],
                send_sem=s_sem.at[side], recv_sem=r_sem.at[1 - side],
                device_id=at(to), device_id_type=MESH,
            ))
        return result

    rims = rim_copies(rim_out, rim_in, rim_send, rim_recv)
    for copy in rims:
        copy.start()

    steps(blocks - 1, ship, early)
    pack(me, arrived)

    ext_rows = lax.broadcasted_iota(jnp.int32, (ext, cells), 0)
    for k in range(6):
        sel = onehot(ext_rows == nb_ref[k:k + 1, :])
        gsel[k, 0:ext, :] = sel
        gsel[k, ext:2 * ext, :] = sel

    flow[...] = jnp.zeros_like(flow)
    slot_id = lax.broadcasted_iota(jnp.int32, (slots, cap), 0).astype(F32) + 1.0

    def unpack(block):
        tile = arrived[block, pieces * layers:pieces * layers + 8, :]
        label = jnp.concatenate([tile[i:i + 1] for i in range(pieces)], axis=1)
        sel = onehot(slot_id == label)
        value = jnp.concatenate(
            [arrived[block, i * layers:(i + 1) * layers, :] for i in range(pieces)], axis=1
        )
        top = value.astype(BF16).astype(F32)
        both = dot_nt(jnp.concatenate([top, value - top], axis=0).astype(BF16), sel)
        flow[...] += both[:layers] + both[layers:]

    unpack(me)

    def take(i):
        block = partner(blocks - offset(i))
        rec_copy(block, block).wait_recv()
        unpack(block)

    before_rims = 2 if blocks == 8 else 0
    for i in range(before_rims):
        take(i)

    for copy in rims:
        copy.wait_recv()

    layer = lax.broadcasted_iota(jnp.int32, (half, cells), 0) + sub * half
    wet = jnp.where(layer < lc_ref[...], 1.0, 0.0)
    layer_f = layer.astype(F32)
    count_ext = jnp.concatenate(
        [count, rim_in[0, rows:rows + 8], rim_in[1, rows:rows + 8]], axis=1
    ).astype(BF16)
    for side in range(2):
        hi, lo = split(rim_in[side, 0:rows])
        first = cells + side * cols
        xa[:, first:first + cols] = hi
        xa[:, ext + first:ext + first + cols] = lo
    for k in range(6):
        pk[k] = dot(xa[...], gsel[k])
        far_count = dot(count_ext, gsel[k, 0:ext])[0:1]
        masks[k] = jnp.where(layer_f < far_count, wet, 0.0)

    steps(blocks - 1, take, before_rims)

    total = jnp.zeros((half, cells), F32)
    for k in range(6):
        u = flow[0:half, k * cells:(k + 1) * cells] * masks[k]
        kap = flow[half:2 * half, k * cells:(k + 1) * cells] * masks[k]
        terms[k] = 0.5 * jnp.abs(u)
        terms[6 + k] = jnp.minimum(u, 0.0) - kap
        total = total + u
    terms[12] = total

    def limiter(t, c):
        q = field[t]
        here = pl.ds(pl.multiple_of(t * half, half), half)
        high = jnp.zeros_like(q)
        low = jnp.zeros_like(q)
        size = jnp.zeros_like(q)
        for k in range(6):
            d = (pk[k, here, :] - q) * masks[k]
            pk[k, here, :] = d
            high = jnp.maximum(high, d)
            low = jnp.minimum(low, d)
            size = size + terms[k] * jnp.abs(d)
        spread = high - low
        lim[here, :] = spread / (spread + size + LIMIT_PAD)
        return c

    groups = lrim_out.shape[0]
    each = tracers // groups
    chunk_rows = each * half
    lrims = []
    for g in range(groups):
        part = slice(g * chunk_rows, (g + 1) * chunk_rows)
        lax.fori_loop(g * each, (g + 1) * each, limiter, 0)
        hi, lo = split(lim[part])
        la[part, 0:cells] = hi
        la[part, ext:ext + cells] = lo
        picked = dot(hi, hsel[0:cells]) + dot(lo, hsel[cells:2 * cells])
        for side in range(2):
            lrim_out[g, side] = picked[:, side * cols:(side + 1) * cols]
        copies = rim_copies(lrim_out.at[g], lrim_in.at[g], lrim_send.at[g], lrim_recv.at[g])
        for copy in copies:
            copy.start()
        lrims.append(copies)

    def advect(t, c):
        q = field[t]
        here = pl.ds(pl.multiple_of(t * half, half), half)
        own_lim = lim[here, :]
        net = q * terms[12]
        for k in range(6):
            bound = jnp.minimum(own_lim, lk[k, here, :])
            net = net + pk[k, here, :] * (terms[6 + k] + bound * terms[k])
        adv[t] = q - net
        return c

    edge_copies = []
    for g in range(groups):
        part = slice(g * chunk_rows, (g + 1) * chunk_rows)
        for copy in lrims[g]:
            copy.wait_recv()
        for side in range(2):
            hi, lo = split(lrim_in[g, side])
            first = cells + side * cols
            la[part, first:first + cols] = hi
            la[part, ext + first:ext + first + cols] = lo
        for k in range(6):
            lk[k, part] = dot(la[part], gsel[k])
        lax.fori_loop(g * each, (g + 1) * each, advect, 0)
        group = slice(g * each, (g + 1) * each)
        edge_out[g] = jnp.where(sub == 0, adv[group, half - 1, :], adv[group, 0, :])
        edge_copy = pltpu.make_async_remote_copy(
            src_ref=edge_out.at[g], dst_ref=edge_in.at[g],
            send_sem=edge_sem.at[g, 0], recv_sem=edge_sem.at[g, 1],
            device_id=other, device_id_type=MESH,
        )
        edge_copy.start()
        edge_copies.append(edge_copy)

    counts = lc_ref[...]
    upper = vd_ref[pl.ds(mine, half), :]
    w_down = jnp.where(
        (layer < layers - 1) & (layer + 1 < counts), upper, 0.0
    )
    cut = jnp.where(half < counts, vd_ref[half - 1:half, :], 0.0)
    row = lax.broadcasted_iota(jnp.int32, (half, cells), 0)
    w_up = jnp.where(row == 0, jnp.where(sub == 0, 0.0, cut), pltpu.roll(w_down, 1, 0))
    light = REACT_RATE * jnp.exp(-3.0 * layer_f / layers) * wet

    def mix(g, i):
        t = g * each + i
        a = adv[t]
        across = edge_in[g, pl.ds(i, 1), :]
        below = jnp.where(row == half - 1, across, pltpu.roll(a, half - 1, 0))
        above = jnp.where(row == 0, across, pltpu.roll(a, 1, 0))
        m = a + w_down * (below - a) - w_up * (a - above)
        adv[t] = m
        sq = m * m
        field[t] = sq / (hs_ref[t] + sq)

    for g in range(groups):
        edge_copies[g].wait()
        for i in range(each):
            mix(g, i)

    def react(t):
        acc = st_ref[t, 0] * field[0]
        for s in range(1, tracers):
            acc = acc + st_ref[t, s] * field[s]
        return adv[t] + light * acc

    def far(i, c):
        res[i] = react((1 - sub) * own + i)
        return c

    def near(i, c):
        out_ref[i, pl.ds(mine, half), :] = react(sub * own + i)
        return c

    lax.fori_loop(0, own, far, 0)
    res_copy = pltpu.make_async_remote_copy(
        src_ref=res, dst_ref=out_ref.at[:, pl.ds(mine, half), :],
        send_sem=res_sem.at[0], recv_sem=res_sem.at[1],
        device_id=other, device_id_type=MESH,
    )
    res_copy.start()
    lax.fori_loop(0, own, near, 0)
    res_copy.wait()

    def drain(i):
        rec_copy(partner(i + 1), me).wait_send()

    steps(blocks - 1, drain)
    for copy in sum(lrims, rims):
        copy.wait_send()


def body(
    tracers, layer_count, neighbor, halo_cells, transport, edge_diff,
    record_dest, record_slot, vert_diff, half_sat, stoich,
):
    own, layers, cells = tracers.shape
    half = layers // 2
    count = 2 * own
    rows = count * half
    cols = halo_cells.shape[1]
    recs = record_dest.shape[0]
    ext = cells + 2 * cols
    n_role = lax.axis_size("role")
    blocks = lax.axis_size("cells") * n_role
    cap = -(-(2 * recs // blocks) // 128) * 128
    packed = cap // LANES * layers + 8
    width = layers + 8
    groups = 4
    vmem = pl.BlockSpec(memory_space=pltpu.VMEM)
    smem = pl.BlockSpec(memory_space=pltpu.SMEM)
    pair = pltpu.SemaphoreType.DMA((2,))
    fours = pltpu.SemaphoreType.DMA((groups, 2))
    return pl.pallas_call(
        functools.partial(kernel, blocks, n_role, cap),
        out_shape=jax.ShapeDtypeStruct(tracers.shape, F32),
        in_specs=[vmem] * 9 + [smem] * 2,
        out_specs=vmem,
        scratch_shapes=[
            pltpu.VMEM((count, half, cells), F32),
            pltpu.VMEM((2 * width, recs), BF16),
            pltpu.VMEM((blocks, packed, LANES), F32),
            pltpu.VMEM((blocks, packed, LANES), F32),
            pltpu.VMEM((layers, 6 * cells), F32),
            pltpu.VMEM((rows, 2 * ext), BF16),
            pltpu.VMEM((rows, 2 * ext), BF16),
            pltpu.VMEM((6, 2 * ext, cells), BF16),
            pltpu.VMEM((2 * cells, 2 * cols), BF16),
            pltpu.VMEM((6, rows, cells), F32),
            pltpu.VMEM((6, rows, cells), F32),
            pltpu.VMEM((rows, cells), F32),
            pltpu.VMEM((count, half, cells), F32),
            pltpu.VMEM((groups, count // groups, cells), F32),
            pltpu.VMEM((groups, count // groups, cells), F32),
            pltpu.VMEM((2, rows + 8, cols), F32),
            pltpu.VMEM((2, rows + 8, cols), F32),
            pltpu.VMEM((groups, 2, rows // groups, cols), F32),
            pltpu.VMEM((groups, 2, rows // groups, cols), F32),
            pltpu.VMEM((own, half, cells), F32),
            pltpu.VMEM((6, half, cells), F32),
            pltpu.VMEM((13, half, cells), F32),
            pltpu.SemaphoreType.DMA((blocks,)),
            pltpu.SemaphoreType.DMA((blocks,)),
            pair, pair, pair, fours, fours, fours, pair,
        ],
        compiler_params=pltpu.CompilerParams(
            collective_id=0, has_side_effects=True, vmem_limit_bytes=52 * 1024 * 1024
        ),
        name="tracer_step",
    )(
        tracers, layer_count.reshape(1, -1), neighbor, halo_cells, transport, edge_diff,
        record_dest.reshape(1, -1), record_slot.reshape(1, -1), vert_diff, half_sat, stoich,
    )


def solution(mesh):
    in_specs = (
        P("sub", None, ("groups", "cells", "role")),
        P(("groups", "cells", "role")),
        P(None, ("groups", "cells", "role")),
        P(None, ("groups", "cells", "role")),
        P("sub", ("groups", "cells", "role")),
        P("sub", ("groups", "cells", "role")),
        P(("groups", "cells", "role")),
        P(("groups", "cells", "role")),
        P(None, ("groups", "cells", "role")),
        P(),
        P(),
    )
    out_specs = P("sub", None, ("groups", "cells", "role"))
    return jax.shard_map(body, mesh=mesh, in_specs=in_specs, out_specs=out_specs, check_vma=False)
```

```python
import functools

import jax
import jax.numpy as jnp
from jax import lax
from jax.experimental import pallas as pl
from jax.experimental.pallas import tpu as pltpu
from jax.sharding import PartitionSpec as P

LIMIT_PAD = 1.5
REACT_RATE = 0.5
F32 = jnp.float32
BF16 = jnp.bfloat16
MESH = pl.DeviceIdType.MESH
NT_DIMS = (((1,), (1,)), ((), ()))


LANES = 128


def steps(count, fn, start=0):
    if count <= 8:
        for i in range(start, count):
            fn(i)
    else:
        lax.fori_loop(start, count, lambda i, c: (fn(i), c)[1], 0)


def dot(a, b):
    return jnp.dot(a, b, preferred_element_type=F32)


def dot_nt(a, b):
    return lax.dot_general(a, b, NT_DIMS, preferred_element_type=F32)


def split(x):
    hi = x.astype(BF16)
    return hi, (x - hi.astype(F32)).astype(BF16)


def onehot(cond):
    return jnp.where(cond, 1.0, 0.0).astype(BF16)


def kernel(
    blocks, n_role, cap,
    tr_ref, lc_ref, nb_ref, halo_ref, tp_ref, ed_ref, dest_ref, slot_ref, vd_ref,
    hs_ref, st_ref,
    out_ref,
    field, rec_a, send, arrived, flow, xa, la, gsel, hsel, pk, lk, lim, adv, edge_out, edge_in,
    rim_out, rim_in, lrim_out, lrim_in, res, masks, terms,
    send_sem, recv_sem, tr_sem, rim_send, rim_recv, lrim_send, lrim_recv, edge_sem, res_sem,
):
    own, layers, cells = tr_ref.shape
    half = layers // 2
    tracers = 2 * own
    rows = tracers * half
    cols = halo_ref.shape[1]
    ext = cells + 2 * cols
    recs = dest_ref.shape[1]
    slots = 6 * cells
    sub = lax.axis_index("sub")
    me = lax.axis_index("cells") * n_role + lax.axis_index("role")
    other = {"sub": 1 - sub}

    def at(block):
        return {"cells": block // n_role, "role": lax.rem(block, n_role)}

    def partner(d):
        return lax.rem(me + d, blocks)

    barrier = pltpu.get_barrier_semaphore()

    def greet(i):
        pl.semaphore_signal(barrier, inc=1, device_id=at(partner(i + 1)), device_id_type=MESH)

    steps(blocks - 1, greet)
    pl.semaphore_signal(barrier, inc=1, device_id=other, device_id_type=MESH)

    mine = pl.multiple_of(sub * half, half)
    theirs = pl.multiple_of((1 - sub) * half, half)

    tr_copy = pltpu.make_async_remote_copy(
        src_ref=tr_ref.at[:, pl.ds(theirs, half), :],
        dst_ref=field.at[pl.ds(sub * own, own)],
        send_sem=tr_sem.at[0], recv_sem=tr_sem.at[1],
        device_id=other, device_id_type=MESH,
    )

    dest = dest_ref[...]
    block_id = lax.broadcasted_iota(jnp.int32, (max(blocks, 8), recs), 0)
    match = jnp.where(block_id == dest, 1.0, 0.0)
    chunk = 256
    before = onehot(
        lax.broadcasted_iota(jnp.int32, (chunk, chunk), 0)
        < lax.broadcasted_iota(jnp.int32, (chunk, chunk), 1)
    )
    carry = jnp.zeros((match.shape[0], 1), F32)
    ranks = []
    for c in range(recs // chunk):
        part = match[:, c * chunk:(c + 1) * chunk]
        rank = dot(part.astype(BF16), before) + carry
        ranks.append(jnp.sum(rank * part, axis=0, keepdims=True))
        carry = carry + jnp.sum(part, axis=1, keepdims=True)
    rank = jnp.concatenate(ranks, axis=1).astype(jnp.int32)
    target = dest * cap + rank

    slot_rows = jnp.broadcast_to(slot_ref[...].astype(F32) + 1.0, (8, recs))
    payload = jnp.concatenate([tp_ref[...], ed_ref[...], slot_rows], axis=0)
    width = payload.shape[0]
    top = payload.astype(BF16).astype(F32)
    rec_a[...] = jnp.concatenate([top, payload - top], axis=0).astype(BF16)

    pl.semaphore_wait(barrier, blocks)
    tr_copy.start()

    place = lax.broadcasted_iota(jnp.int32, (cap, recs), 0)

    pieces = cap // LANES
    slot_row = lax.broadcasted_iota(jnp.int32, (8, LANES), 0)

    def pack(block, ref):
        sel = onehot(place == target - block * cap)
        both = dot_nt(rec_a[...], sel)
        got = both[:width] + both[width:]
        tile = jnp.zeros((8, LANES), F32)
        for i in range(pieces):
            piece = slice(i * LANES, (i + 1) * LANES)
            ref[block, i * layers:(i + 1) * layers, :] = got[:layers, piece]
            tile = jnp.where(slot_row == i, got[layers:layers + 8, piece], tile)
        ref[block, pieces * layers:pieces * layers + 8, :] = tile

    def rec_copy(block, source):
        return pltpu.make_async_remote_copy(
            src_ref=send.at[block], dst_ref=arrived.at[source],
            send_sem=send_sem.at[block], recv_sem=recv_sem.at[source],
            device_id=at(block), device_id_type=MESH,
        )

    order = (4, 3, 5, 2, 6, 1, 7)

    def offset(i):
        return order[i] if blocks == 8 else i + 1

    def ship(i):
        block = partner(offset(i))
        pack(block, send)
        rec_copy(block, me).start()

    early = 3 if blocks == 8 else 0
    for i in range(early):
        ship(i)

    local_rows = lax.broadcasted_iota(jnp.int32, (cells, cols), 0)
    for side in range(2):
        sel = onehot(local_rows == halo_ref[side:side + 1, :])
        hsel[0:cells, side * cols:(side + 1) * cols] = sel
        hsel[cells:2 * cells, side * cols:(side + 1) * cols] = sel

    field[pl.ds(sub * own, own)] = tr_ref[:, pl.ds(mine, half), :]
    tr_copy.wait()
    whole = field[...].reshape(rows, cells)
    hi, lo = split(whole)
    xa[:, 0:cells] = hi
    xa[:, ext:ext + cells] = lo
    picked = dot(hi, hsel[0:cells]) + dot(lo, hsel[cells:2 * cells])
    count = jnp.broadcast_to(lc_ref[...].astype(F32), (8, cells))
    picked_count = dot(count.astype(BF16), hsel[0:cells])
    for side in range(2):
        rim_out[side, 0:rows] = picked[:, side * cols:(side + 1) * cols]
        rim_out[side, rows:rows + 8] = picked_count[:, side * cols:(side + 1) * cols]

    def rim_copies(out, into, s_sem, r_sem):
        result = []
        for side in range(2):
            to = partner(blocks - 1 if side == 0 else 1)
            result.append(pltpu.make_async_remote_copy(
                src_ref=out.at[side], dst_ref=into.at[1 - side],
                send_sem=s_sem.at[side], recv_sem=r_sem.at[1 - side],
                device_id=at(to), device_id_type=MESH,
            ))
        return result

    rims = rim_copies(rim_out, rim_in, rim_send, rim_recv)
    for copy in rims:
        copy.start()

    steps(blocks - 1, ship, early)
    pack(me, arrived)

    ext_rows = lax.broadcasted_iota(jnp.int32, (ext, cells), 0)
    for k in range(6):
        sel = onehot(ext_rows == nb_ref[k:k + 1, :])
        gsel[k, 0:ext, :] = sel
        gsel[k, ext:2 * ext, :] = sel

    flow[...] = jnp.zeros_like(flow)
    slot_id = lax.broadcasted_iota(jnp.int32, (slots, cap), 0).astype(F32) + 1.0

    def unpack(block):
        tile = arrived[block, pieces * layers:pieces * layers + 8, :]
        label = jnp.concatenate([tile[i:i + 1] for i in range(pieces)], axis=1)
        sel = onehot(slot_id == label)
        value = jnp.concatenate(
            [arrived[block, i * layers:(i + 1) * layers, :] for i in range(pieces)], axis=1
        )
        top = value.astype(BF16).astype(F32)
        both = dot_nt(jnp.concatenate([top, value - top], axis=0).astype(BF16), sel)
        flow[...] += both[:layers] + both[layers:]

    unpack(me)

    def take(i):
        block = partner(blocks - offset(i))
        rec_copy(block, block).wait_recv()
        unpack(block)

    before_rims = 2 if blocks == 8 else 0
    for i in range(before_rims):
        take(i)

    for copy in rims:
        copy.wait_recv()

    layer = lax.broadcasted_iota(jnp.int32, (half, cells), 0) + sub * half
    wet = jnp.where(layer < lc_ref[...], 1.0, 0.0)
    layer_f = layer.astype(F32)
    count_ext = jnp.concatenate(
        [count, rim_in[0, rows:rows + 8], rim_in[1, rows:rows + 8]], axis=1
    ).astype(BF16)
    for side in range(2):
        hi, lo = split(rim_in[side, 0:rows])
        first = cells + side * cols
        xa[:, first:first + cols] = hi
        xa[:, ext + first:ext + first + cols] = lo
    for k in range(6):
        pk[k] = dot(xa[...], gsel[k])
        far_count = dot(count_ext, gsel[k, 0:ext])[0:1]
        masks[k] = jnp.where(layer_f < far_count, wet, 0.0)

    steps(blocks - 1, take, before_rims)

    total = jnp.zeros((half, cells), F32)
    for k in range(6):
        u = flow[0:half, k * cells:(k + 1) * cells] * masks[k]
        kap = flow[half:2 * half, k * cells:(k + 1) * cells] * masks[k]
        terms[k] = 0.5 * jnp.abs(u)
        terms[6 + k] = jnp.minimum(u, 0.0) - kap
        total = total + u
    terms[12] = total

    def limiter(t, c):
        q = field[t]
        here = pl.ds(pl.multiple_of(t * half, half), half)
        high = jnp.zeros_like(q)
        low = jnp.zeros_like(q)
        size = jnp.zeros_like(q)
        for k in range(6):
            d = (pk[k, here, :] - q) * masks[k]
            pk[k, here, :] = d
            high = jnp.maximum(high, d)
            low = jnp.minimum(low, d)
            size = size + terms[k] * jnp.abs(d)
        spread = high - low
        lim[here, :] = spread / (spread + size + LIMIT_PAD)
        return c

    groups = lrim_out.shape[0]
    each = tracers // groups
    chunk_rows = each * half
    lrims = []
    for g in range(groups):
        part = slice(g * chunk_rows, (g + 1) * chunk_rows)
        lax.fori_loop(g * each, (g + 1) * each, limiter, 0)
        hi, lo = split(lim[part])
        la[part, 0:cells] = hi
        la[part, ext:ext + cells] = lo
        picked = dot(hi, hsel[0:cells]) + dot(lo, hsel[cells:2 * cells])
        for side in range(2):
            lrim_out[g, side] = picked[:, side * cols:(side + 1) * cols]
        copies = rim_copies(lrim_out.at[g], lrim_in.at[g], lrim_send.at[g], lrim_recv.at[g])
        for copy in copies:
            copy.start()
        lrims.append(copies)

    def advect(t, c):
        q = field[t]
        here = pl.ds(pl.multiple_of(t * half, half), half)
        own_lim = lim[here, :]
        net = q * terms[12]
        for k in range(6):
            bound = jnp.minimum(own_lim, lk[k, here, :])
            net = net + pk[k, here, :] * (terms[6 + k] + bound * terms[k])
        adv[t] = q - net
        return c

    edge_copies = []
    for g in range(groups):
        part = slice(g * chunk_rows, (g + 1) * chunk_rows)
        for copy in lrims[g]:
            copy.wait_recv()
        for side in range(2):
            hi, lo = split(lrim_in[g, side])
            first = cells + side * cols
            la[part, first:first + cols] = hi
            la[part, ext + first:ext + first + cols] = lo
        for k in range(6):
            lk[k, part] = dot(la[part], gsel[k])
        lax.fori_loop(g * each, (g + 1) * each, advect, 0)
        group = slice(g * each, (g + 1) * each)
        edge_out[g] = jnp.where(sub == 0, adv[group, half - 1, :], adv[group, 0, :])
        edge_copy = pltpu.make_async_remote_copy(
            src_ref=edge_out.at[g], dst_ref=edge_in.at[g],
            send_sem=edge_sem.at[g, 0], recv_sem=edge_sem.at[g, 1],
            device_id=other, device_id_type=MESH,
        )
        edge_copy.start()
        edge_copies.append(edge_copy)

    counts = lc_ref[...]
    upper = vd_ref[pl.ds(mine, half), :]
    w_down = jnp.where(
        (layer < layers - 1) & (layer + 1 < counts), upper, 0.0
    )
    cut = jnp.where(half < counts, vd_ref[half - 1:half, :], 0.0)
    row = lax.broadcasted_iota(jnp.int32, (half, cells), 0)
    w_up = jnp.where(row == 0, jnp.where(sub == 0, 0.0, cut), pltpu.roll(w_down, 1, 0))
    light = REACT_RATE * jnp.exp(-3.0 * layer_f / layers) * wet

    def mix(g, i):
        t = g * each + i
        a = adv[t]
        across = edge_in[g, pl.ds(i, 1), :]
        below = jnp.where(row == half - 1, across, pltpu.roll(a, half - 1, 0))
        above = jnp.where(row == 0, across, pltpu.roll(a, 1, 0))
        m = a + w_down * (below - a) - w_up * (a - above)
        adv[t] = m
        sq = m * m
        field[t] = sq / (hs_ref[t] + sq)

    for g in range(groups):
        edge_copies[g].wait()
        for i in range(each):
            mix(g, i)

    def react(t):
        acc = st_ref[t, 0] * field[0]
        for s in range(1, tracers):
            acc = acc + st_ref[t, s] * field[s]
        return adv[t] + light * acc

    def far(i, c):
        res[i] = react((1 - sub) * own + i)
        return c

    def near(i, c):
        out_ref[i, pl.ds(mine, half), :] = react(sub * own + i)
        return c

    lax.fori_loop(0, own, far, 0)
    res_copy = pltpu.make_async_remote_copy(
        src_ref=res, dst_ref=out_ref.at[:, pl.ds(mine, half), :],
        send_sem=res_sem.at[0], recv_sem=res_sem.at[1],
        device_id=other, device_id_type=MESH,
    )
    res_copy.start()
    lax.fori_loop(0, own, near, 0)
    res_copy.wait()

    def drain(i):
        rec_copy(partner(i + 1), me).wait_send()

    steps(blocks - 1, drain)
    for copy in sum(lrims, rims):
        copy.wait_send()


def body(
    tracers, layer_count, neighbor, halo_cells, transport, edge_diff,
    record_dest, record_slot, vert_diff, half_sat, stoich,
):
    own, layers, cells = tracers.shape
    half = layers // 2
    count = 2 * own
    rows = count * half
    cols = halo_cells.shape[1]
    recs = record_dest.shape[0]
    ext = cells + 2 * cols
    n_role = lax.axis_size("role")
    blocks = lax.axis_size("cells") * n_role
    cap = -(-(2 * recs // blocks) // 128) * 128
    packed = cap // LANES * layers + 8
    width = layers + 8
    groups = 4
    vmem = pl.BlockSpec(memory_space=pltpu.VMEM)
    smem = pl.BlockSpec(memory_space=pltpu.SMEM)
    pair = pltpu.SemaphoreType.DMA((2,))
    fours = pltpu.SemaphoreType.DMA((groups, 2))
    return pl.pallas_call(
        functools.partial(kernel, blocks, n_role, cap),
        out_shape=jax.ShapeDtypeStruct(tracers.shape, F32),
        in_specs=[vmem] * 9 + [smem] * 2,
        out_specs=vmem,
        scratch_shapes=[
            pltpu.VMEM((count, half, cells), F32),
            pltpu.VMEM((2 * width, recs), BF16),
            pltpu.VMEM((blocks, packed, LANES), F32),
            pltpu.VMEM((blocks, packed, LANES), F32),
            pltpu.VMEM((layers, 6 * cells), F32),
            pltpu.VMEM((rows, 2 * ext), BF16),
            pltpu.VMEM((rows, 2 * ext), BF16),
            pltpu.VMEM((6, 2 * ext, cells), BF16),
            pltpu.VMEM((2 * cells, 2 * cols), BF16),
            pltpu.VMEM((6, rows, cells), F32),
            pltpu.VMEM((6, rows, cells), F32),
            pltpu.VMEM((rows, cells), F32),
            pltpu.VMEM((count, half, cells), F32),
            pltpu.VMEM((groups, count // groups, cells), F32),
            pltpu.VMEM((groups, count // groups, cells), F32),
            pltpu.VMEM((2, rows + 8, cols), F32),
            pltpu.VMEM((2, rows + 8, cols), F32),
            pltpu.VMEM((groups, 2, rows // groups, cols), F32),
            pltpu.VMEM((groups, 2, rows // groups, cols), F32),
            pltpu.VMEM((own, half, cells), F32),
            pltpu.VMEM((6, half, cells), F32),
            pltpu.VMEM((13, half, cells), F32),
            pltpu.SemaphoreType.DMA((blocks,)),
            pltpu.SemaphoreType.DMA((blocks,)),
            pair, pair, pair, fours, fours, fours, pair,
        ],
        compiler_params=pltpu.CompilerParams(
            collective_id=0, has_side_effects=True, vmem_limit_bytes=52 * 1024 * 1024
        ),
        name="tracer_step",
    )(
        tracers, layer_count.reshape(1, -1), neighbor, halo_cells, transport, edge_diff,
        record_dest.reshape(1, -1), record_slot.reshape(1, -1), vert_diff, half_sat, stoich,
    )


def solution(mesh):
    in_specs = (
        P("sub", None, ("groups", "cells", "role")),
        P(("groups", "cells", "role")),
        P(None, ("groups", "cells", "role")),
        P(None, ("groups", "cells", "role")),
        P("sub", ("groups", "cells", "role")),
        P("sub", ("groups", "cells", "role")),
        P(("groups", "cells", "role")),
        P(("groups", "cells", "role")),
        P(None, ("groups", "cells", "role")),
        P(),
        P(),
    )
    out_specs = P("sub", None, ("groups", "cells", "role"))
    return jax.shard_map(body, mesh=mesh, in_specs=in_specs, out_specs=out_specs, check_vma=False)
```
